256 devices in a mesh: row: 16 (over z, core), col: 4 (over x), layer: 4 (over y).
Axes of the slice: x: 4, y: 4, z: 8, core: 2. Of those that a mesh axis runs over, the one named last changes fastest.
Arguments:
- density: bfloat16 [4096, 4096], P('row', 'col'), as said below
- pattern: int32 [64, 64], replicated, may hold values from 0 to 1, as said below
- branches: int32 [4], replicated, may hold values from 0 to 1, as said below
- basis: bfloat16 [4096, 128], replicated, may hold values from -3 to 3
- brick_list: int32 [64, 8], replicated, may hold values from 0 to 255
Outputs:
- purified: bfloat16 [4096, 4096], P('row', 'col')
- grid_density: float32 [16, 4, 4, 128], P('row', 'col', 'layer')
The draws below stay inside these ranges and needn't reach their ends.
Inputs may be any that keep to these rules, and one draw needn't show every extreme that they name: `pattern`: symmetric, ones on the diagonal. `density`: symmetric, zero outside the blocks that pattern marks. `branches`: both values occur.
All inputs are finite; a program needn't handle non-finite values.
Results may differ from the reference program's by a relative error of at most 0.013.
The reference program's roundings to bfloat16 on the way count: a program that leaves them out, or rounds other values in their place, can miss the bound.
Values may be sent and summed in bfloat16 or wider, within the bound.
No kernel may reach another device: no remote copies, remote signals or barrier semaphores. Data moves between devices by JAX's collectives and lax.ppermute only.
A program may use at most 64 MiB of HBM per device.

```python
import jax
import jax.numpy as jnp
from jax import lax

DB = 64
NB = 64
CB = 128
SPREAD = 8
STEPS = 4
N = 4096
N_ROW = 16
N_COL = 4
N_LAYER = 4


def pattern_from(key):
    sub_key = jax.random.fold_in(key, 11)
    index = jnp.arange(NB, dtype=jnp.int32)
    jitter = jax.random.randint(sub_key, (3, NB), 0, 2).astype(jnp.int32)
    place_x = 2 * (index % 4) + jitter[0]
    place_y = 2 * (index // 4 % 4) + jitter[1]
    place_z = 2 * (index // 16) + jitter[2]
    apart = (place_x[:, None] - place_x[None, :]) ** 2 + (place_y[:, None] - place_y[None, :]) ** 2 + (place_z[:, None] - place_z[None, :]) ** 2
    near = (apart <= 9).astype(jnp.int32)
    upper = jnp.triu(near, 1)
    return upper + upper.T + jnp.eye(NB, dtype=jnp.int32)


def draw_pattern(key, part):
    return pattern_from(key)


def draw_branches(key, part):
    key = jax.random.fold_in(key, 17)
    values = jax.random.randint(key, (STEPS,), 0, 2).astype(jnp.int32)
    return values.at[0].set(1 - values[1]).astype(jnp.int32)


def draw_brick_list(key, part):
    key = jax.random.fold_in(key, 5)
    key_x, key_y, key_z = jax.random.split(key, 3)
    centre_x = jax.random.randint(key_x, (NB,), 0, N_ROW).astype(jnp.int32).at[0].set(N_ROW - 1)
    centre_y = jax.random.randint(key_y, (NB,), 0, N_COL).astype(jnp.int32).at[0].set(N_COL - 1)
    centre_z = jax.random.randint(key_z, (NB,), 0, N_LAYER).astype(jnp.int32).at[0].set(N_LAYER - 1)
    offsets = jnp.arange(SPREAD, dtype=jnp.int32)
    brick_x = (centre_x[:, None] + offsets[None, :] // 4 % 2) % N_ROW
    brick_y = (centre_y[:, None] + offsets[None, :] // 2 % 2) % N_COL
    brick_z = (centre_z[:, None] + offsets[None, :] % 2) % N_LAYER
    return ((brick_x * N_COL + brick_y) * N_LAYER + brick_z).astype(jnp.int32)


def draw_density(key, part):
    blocks = pattern_from(key)
    key = jax.random.fold_in(key, 3)
    key_one, key_two = jax.random.split(key, 2)
    mask = jnp.repeat(jnp.repeat(blocks.astype(jnp.float32), DB, 0), DB, 1)
    diagonal_values = jax.random.uniform(key_two, (N,), jnp.float32, 0.0, 1.0)
    noise = jax.random.normal(key_one, (N, N), jnp.float32)
    symmetric = (noise + noise.T) * (0.5 / jnp.sqrt(jnp.float32(N)))
    offdiag = symmetric * mask * (1.0 - jnp.eye(N, dtype=jnp.float32))
    return (offdiag + jnp.diag(diagonal_values)).astype(jnp.bfloat16)


def scatter_about(rng, dims, deviation, limit, held_as=jnp.bfloat16):
    entries = deviation * jax.random.normal(rng, dims, jnp.float32)
    return jnp.clip(entries, min=-limit, max=limit).astype(held_as)


def setup_inputs(seed: int = 0) -> dict:
    splits = jax.random.split(jax.random.key(seed), 6)
    return {
        "density": draw_density(jax.random.fold_in(splits[5], 71), 0),
        "pattern": draw_pattern(jax.random.fold_in(splits[5], 71), 0),
        "branches": draw_branches(jax.random.fold_in(splits[5], 71), 0),
        "basis": scatter_about(splits[3], (N, CB), 0.5, 3.0),
        "brick_list": draw_brick_list(jax.random.fold_in(splits[5], 71), 0),
    }


def reference(density, pattern, branches, basis, brick_list):
    mask = jnp.repeat(jnp.repeat(pattern.astype(jnp.float32), DB, 0), DB, 1)
    current = density
    for number in range(STEPS):
        square = jnp.dot(current, current, preferred_element_type=jnp.float32)
        previous = current.astype(jnp.float32)
        updated = jnp.where(branches[number] == 0, square, 2.0 * previous - square)
        current = (updated * mask).astype(jnp.bfloat16)
    orbital = jnp.arange(N, dtype=jnp.int32)
    owner = brick_list[orbital // DB, orbital % SPREAD]
    same = owner[:, None] == owner[None, :]
    kept = jnp.where(same, current, jnp.zeros((), current.dtype))
    orbital_field = lax.dot_general(kept, basis, (((0,), (0,)), ((), ())), preferred_element_type=jnp.float32)
    weights = orbital_field * basis.astype(jnp.float32)
    grid = jax.ops.segment_sum(weights, owner, num_segments=N_ROW * N_COL * N_LAYER)
    return current, grid.reshape(N_ROW, N_COL, N_LAYER, CB)
```

```python
import functools

import jax
import jax.numpy as jnp
from jax import lax
from jax.experimental import pallas as pl
from jax.experimental.pallas import tpu as pltpu
from jax.sharding import PartitionSpec as P

DB = 64
STEPS = 4
TILE = 256
NZ, NX, NY = 8, 4, 4
PANELS = 16
CB = 128
BRICKS = 256
AXES = ("row", "col", "layer")


def device_number(z, core, x, y):
    return (((z % NZ) * 2 + core) * NX + x % NX) * NY + y % NY


def pairs(move):
    return [
        (device_number(z, core, x, y), device_number(*move(z, core, x, y)))
        for z in range(NZ)
        for core in range(2)
        for x in range(NX)
        for y in range(NY)
    ]


def first_leg(hops):
    return pairs(lambda z, c, x, y: (z, c, x + hops * (1 - c), y + hops * c))


def second_leg(hops):
    return pairs(lambda z, c, x, y: (z, c, x + hops * c, y + hops * (1 - c)))


def along_z(hops):
    return pairs(lambda z, c, x, y: (z + hops * (1 - 2 * c), c, x, y))


def other_core():
    return pairs(lambda z, c, x, y: (z, 1 - c, x, y))


def mask_strip(pattern_ref, block_row, first_block):
    lane_block = lax.broadcasted_iota(jnp.int32, (1, TILE), 1) // DB
    strip = jnp.zeros((1, TILE), jnp.float32)
    for block in range(TILE // DB):
        keep = pattern_ref[block_row, first_block + block].astype(jnp.float32)
        strip = jnp.where(lane_block == block, keep, strip)
    return strip


def step_kernel(number, last, *refs):
    (place_ref, branches_ref, pattern_ref, own_ref, r0, r1, r2, r3,
     own_swap, n1, n2, n3, n4, f1, f2, f3, f4) = refs[:17]
    refs = refs[17:]
    if last:
        row_owner_ref, col_owner_ref, row_basis_ref, col_basis_ref = refs[:4]
        out_ref, bricks_ref, column_ref, sems = refs[4:]
    else:
        out_ref, column_ref, sems = refs
    z, core, x, y = place_ref[0], place_ref[1], place_ref[2], place_ref[3]
    side = 2 * core - 1
    copies = []

    def put(source, offset, which_core):
        slot = ((z + offset + NZ) % NZ) * 2 + which_core
        copy = pltpu.make_async_copy(source, column_ref.at[slot], sems.at[len(copies)])
        copy.start()
        copies.append(copy)

    other = 1 - core
    put(own_ref, 0, core)
    put(own_swap, 0, other)
    for distance, near, far in ((1, n1, f1), (2, n2, f2), (3, n3, f3)):
        put(near.at[0], side * distance, core)
        put(near.at[1], side * distance, other)
        put(far.at[0], -side * distance, other)
        put(far.at[1], -side * distance, core)
    put(n4, 4, core)
    put(f4, 4, other)
    for copy in copies:
        copy.wait()
    total = None
    for second, part in enumerate((r0, r1, r2, r3)):
        for first in range(4):
            back_x = jnp.where(core == 0, first, second)
            back_y = jnp.where(core == 0, second, first)
            k = ((x - back_x + NX) % NX) * NY + (y - back_y + NY) % NY
            term = jnp.dot(part[first], column_ref[k], preferred_element_type=jnp.float32)
            total = term if total is None else total + term
    previous = own_ref[...].astype(jnp.float32)
    updated = jnp.where(branches_ref[number] == 0, total, 2.0 * previous - total)
    row_block = (z * 2 + core) * (TILE // DB)
    col_block = (x * NY + y) * (TILE // DB)
    for block in range(TILE // DB):
        rows = pl.ds(block * DB, DB)
        strip = mask_strip(pattern_ref, row_block + block, col_block)
        out_ref[rows, :] = (updated[block * DB:(block + 1) * DB] * strip).astype(jnp.bfloat16)
    if last:
        same = row_owner_ref[...] == col_owner_ref[...]
        kept = jnp.where(same, out_ref[...].astype(jnp.float32), 0.0).astype(jnp.bfloat16)
        field = lax.dot_general(
            kept, row_basis_ref[...], (((0,), (0,)), ((), ())), preferred_element_type=jnp.float32
        )
        weights = field * col_basis_ref[...].astype(jnp.float32)
        number_of = lax.broadcasted_iota(jnp.int32, (BRICKS, TILE), 0)
        one_hot = (number_of == col_owner_ref[...]).astype(jnp.float32)
        bricks_ref[...] = jnp.dot(
            one_hot, weights, precision=lax.Precision.HIGHEST, preferred_element_type=jnp.float32
        )


def run_step(number, last, place, branches, pattern, own, rows, columns, extra):
    smem = pl.BlockSpec(memory_space=pltpu.SMEM)
    vmem = pl.BlockSpec(memory_space=pltpu.VMEM)
    anywhere = pl.BlockSpec(memory_space=pl.ANY)
    out_shape = [jax.ShapeDtypeStruct((TILE, TILE), jnp.bfloat16)]
    if last:
        out_shape.append(jax.ShapeDtypeStruct((BRICKS, CB), jnp.float32))
    return pl.pallas_call(
        functools.partial(step_kernel, number, last),
        out_shape=out_shape,
        in_specs=[smem] * 3 + [vmem] * 5 + [anywhere] * 9 + [vmem] * len(extra),
        out_specs=[vmem] * len(out_shape),
        scratch_shapes=[
            pltpu.VMEM((PANELS, TILE, TILE), jnp.bfloat16),
            pltpu.SemaphoreType.DMA((PANELS,)),
        ],
        compiler_params=pltpu.CompilerParams(vmem_limit_bytes=24 << 20),
        cost_estimate=pl.CostEstimate(
            flops=2 * TILE * TILE * 4096, bytes_accessed=4 << 20, transcendentals=0
        ),
        name="square_last" if last else "square",
    )(place, branches, pattern, own, *rows, *columns, *extra)


def move(value, route):
    return lax.ppermute(value, AXES, route)


def gather_rows(own):
    first = jnp.stack([own] + [move(own, first_leg(hops)) for hops in (1, 2, 3)])
    return [first] + [move(first, second_leg(hops)) for hops in (1, 2, 3)]


def gather_columns(own):
    own_swap = move(own, other_core())
    pair = jnp.stack([own, own_swap])
    n1 = move(pair, along_z(1))
    n2 = move(pair, along_z(2))
    n3 = move(n2, along_z(1))
    n4 = move(n2[0], along_z(2))
    far = [move(near, other_core()) for near in (n1, n2, n3, n4)]
    return [own_swap, n1, n2, n3, n4] + far


def on_device(density, pattern, branches, basis, brick_list):
    row = lax.axis_index("row")
    col = lax.axis_index("col")
    layer = lax.axis_index("layer")
    place = jnp.stack([row // 2, row % 2, col, layer]).astype(jnp.int32)
    own = lax.dynamic_slice_in_dim(density, layer * TILE, TILE, 1)
    panel = col * NY + layer
    owners = jnp.tile(brick_list, (1, DB // brick_list.shape[1])).reshape(-1)
    extra = (
        lax.dynamic_slice_in_dim(owners, row * TILE, TILE, 0)[:, None],
        lax.dynamic_slice_in_dim(owners, panel * TILE, TILE, 0)[None, :],
        lax.dynamic_slice_in_dim(basis, row * TILE, TILE, 0),
        lax.dynamic_slice_in_dim(basis, panel * TILE, TILE, 0),
    )
    for number in range(STEPS):
        last = number == STEPS - 1
        out = run_step(
            number, last, place, branches, pattern, own, gather_rows(own), gather_columns(own),
            extra if last else (),
        )
        own = out[0]
    purified = lax.all_gather(own, "layer", axis=1, tiled=True)
    bricks = out[1].reshape(PANELS, PANELS, CB)
    bricks = lax.all_to_all(bricks, "row", 0, 0).sum(0)
    bricks = lax.all_to_all(bricks, ("col", "layer"), 0, 0, tiled=True).sum(0)
    return (purified, bricks.reshape(1, 1, 1, -1))


def solution(mesh):
    placed = (P("row", "col"), P(), P(), P(), P())
    return jax.shard_map(
        on_device,
        mesh=mesh,
        in_specs=placed,
        out_specs=(P("row", "col"), P("row", "col", "layer", None)),
        check_vma=False,
    )
```

```python
import functools

import jax
import jax.numpy as jnp
from jax import lax
from jax.experimental import pallas as pl
from jax.experimental.pallas import tpu as pltpu
from jax.sharding import PartitionSpec as P

DB = 64
STEPS = 4
TILE = 256
NZ, NX, NY = 8, 4, 4
PANELS = 16
CB = 128
BRICKS = 256
AXES = ("row", "col", "layer")


def device_number(z, core, x, y):
    return (((z % NZ) * 2 + core) * NX + x % NX) * NY + y % NY


def pairs(move):
    return [
        (device_number(z, core, x, y), device_number(*move(z, core, x, y)))
        for z in range(NZ)
        for core in range(2)
        for x in range(NX)
        for y in range(NY)
    ]


def first_leg(hops):
    return pairs(lambda z, c, x, y: (z, c, x + hops * (1 - c), y + hops * c))


def second_leg(hops):
    return pairs(lambda z, c, x, y: (z, c, x + hops * c, y + hops * (1 - c)))


def along_z(hops):
    return pairs(lambda z, c, x, y: (z + hops * (1 - 2 * c), c, x, y))


def other_core():
    return pairs(lambda z, c, x, y: (z, 1 - c, x, y))


def mask_strip(pattern_ref, block_row, first_block):
    lane_block = lax.broadcasted_iota(jnp.int32, (1, TILE), 1) // DB
    strip = jnp.zeros((1, TILE), jnp.float32)
    for block in range(TILE // DB):
        keep = pattern_ref[block_row, first_block + block].astype(jnp.float32)
        strip = jnp.where(lane_block == block, keep, strip)
    return strip


def step_kernel(number, last, *refs):
    (place_ref, branches_ref, pattern_ref, own_ref, r0, r1, r2, r3,
     own_swap, n1, n2, n3, n4, f1, f2, f3, f4) = refs[:17]
    refs = refs[17:]
    if last:
        row_owner_ref, col_owner_ref, row_basis_ref, col_basis_ref = refs[:4]
        out_ref, bricks_ref, column_ref, row_ref, column_sems, row_sems = refs[4:]
    else:
        out_ref, column_ref, row_ref, column_sems, row_sems = refs
    z, core, x, y = place_ref[0], place_ref[1], place_ref[2], place_ref[3]
    side = 2 * core - 1
    copies = []

    def put(source, offset, which_core):
        slot = ((z + offset + NZ) % NZ) * 2 + which_core
        copy = pltpu.make_async_copy(source, column_ref.at[slot], column_sems.at[len(copies)])
        copy.start()
        copies.append(copy)

    other = 1 - core
    put(own_ref, 0, core)
    put(own_swap, 0, other)
    for distance, near, far in ((1, n1, f1), (2, n2, f2), (3, n3, f3)):
        put(near.at[0], side * distance, core)
        put(near.at[1], side * distance, other)
        put(far.at[0], -side * distance, other)
        put(far.at[1], -side * distance, core)
    put(n4, 4, core)
    put(f4, 4, other)
    row_copies = []
    for second, part in enumerate((r0, r1, r2, r3)):
        copy = pltpu.make_async_copy(part, row_ref.at[second], row_sems.at[second])
        copy.start()
        row_copies.append(copy)
    for copy in copies:
        copy.wait()
    total = None
    for second in range(4):
        row_copies[second].wait()
        for first in range(4):
            back_x = jnp.where(core == 0, first, second)
            back_y = jnp.where(core == 0, second, first)
            k = ((x - back_x + NX) % NX) * NY + (y - back_y + NY) % NY
            term = jnp.dot(
                row_ref[second, first], column_ref[k], preferred_element_type=jnp.float32
            )
            total = term if total is None else total + term
    previous = own_ref[...].astype(jnp.float32)
    updated = jnp.where(branches_ref[number] == 0, total, 2.0 * previous - total)
    row_block = (z * 2 + core) * (TILE // DB)
    col_block = (x * NY + y) * (TILE // DB)
    for block in range(TILE // DB):
        rows = pl.ds(block * DB, DB)
        strip = mask_strip(pattern_ref, row_block + block, col_block)
        out_ref[rows, :] = (updated[block * DB:(block + 1) * DB] * strip).astype(jnp.bfloat16)
    if last:
        same = row_owner_ref[...] == col_owner_ref[...]
        kept = jnp.where(same, out_ref[...].astype(jnp.float32), 0.0).astype(jnp.bfloat16)
        field = lax.dot_general(
            kept, row_basis_ref[...], (((0,), (0,)), ((), ())), preferred_element_type=jnp.float32
        )
        weights = field * col_basis_ref[...].astype(jnp.float32)
        number_of = lax.broadcasted_iota(jnp.int32, (BRICKS, TILE), 0)
        one_hot = (number_of == col_owner_ref[...]).astype(jnp.float32)
        bricks_ref[...] = jnp.dot(
            one_hot, weights, precision=lax.Precision.HIGHEST, preferred_element_type=jnp.float32
        )


def join_kernel(place_ref, t0, t1, t2, t3, out_ref, sems):
    y = place_ref[3]
    copies = []
    for back, part in enumerate((t0, t1, t2, t3)):
        start = pl.multiple_of(((y - back + NY) % NY) * TILE, TILE)
        copy = pltpu.make_async_copy(part, out_ref.at[:, pl.ds(start, TILE)], sems.at[back])
        copy.start()
        copies.append(copy)
    for copy in copies:
        copy.wait()


def join_layers(place, parts):
    return pl.pallas_call(
        join_kernel,
        out_shape=jax.ShapeDtypeStruct((TILE, NY * TILE), jnp.bfloat16),
        in_specs=[pl.BlockSpec(memory_space=pltpu.SMEM)] + [pl.BlockSpec(memory_space=pl.ANY)] * 4,
        out_specs=pl.BlockSpec(memory_space=pl.ANY),
        scratch_shapes=[pltpu.SemaphoreType.DMA((NY,))],
        name="join_layers",
    )(place, *parts)


def run_step(number, last, place, branches, pattern, own, rows, columns, extra):
    smem = pl.BlockSpec(memory_space=pltpu.SMEM)
    vmem = pl.BlockSpec(memory_space=pltpu.VMEM)
    anywhere = pl.BlockSpec(memory_space=pl.ANY)
    out_shape = [jax.ShapeDtypeStruct((TILE, TILE), jnp.bfloat16)]
    if last:
        out_shape.append(jax.ShapeDtypeStruct((BRICKS, CB), jnp.float32))
    return pl.pallas_call(
        functools.partial(step_kernel, number, last),
        out_shape=out_shape,
        in_specs=[smem] * 3 + [vmem] + [anywhere] * 13 + [vmem] * len(extra),
        out_specs=[vmem] * len(out_shape),
        scratch_shapes=[
            pltpu.VMEM((PANELS, TILE, TILE), jnp.bfloat16),
            pltpu.VMEM((4, 4, TILE, TILE), jnp.bfloat16),
            pltpu.SemaphoreType.DMA((PANELS,)),
            pltpu.SemaphoreType.DMA((4,)),
        ],
        compiler_params=pltpu.CompilerParams(vmem_limit_bytes=24 << 20),
        cost_estimate=pl.CostEstimate(
            flops=2 * TILE * TILE * 4096, bytes_accessed=4 << 20, transcendentals=0
        ),
        name="square_last" if last else "square",
    )(place, branches, pattern, own, *rows, *columns, *extra)


def move(value, route):
    return lax.ppermute(value, AXES, route)


def gather_rows(own):
    first = jnp.stack([own] + [move(own, first_leg(hops)) for hops in (1, 2, 3)])
    return [first] + [move(first, second_leg(hops)) for hops in (1, 2, 3)]


def gather_columns(own, first):
    own_swap = move(own, other_core())
    pair = jnp.stack([own, own_swap])
    n1 = move(pair, along_z(1))
    n2 = move(pair, along_z(2))
    later, _ = lax.optimization_barrier((n2, first))
    n3 = move(later, along_z(1))
    n4 = move(later[0], along_z(2))
    far = [move(near, other_core()) for near in (n1, n2, n3, n4)]
    return [own_swap, n1, n2, n3, n4] + far


def on_device(density, pattern, branches, basis, brick_list):
    row = lax.axis_index("row")
    col = lax.axis_index("col")
    layer = lax.axis_index("layer")
    place = jnp.stack([row // 2, row % 2, col, layer]).astype(jnp.int32)
    own = lax.dynamic_slice_in_dim(density, layer * TILE, TILE, 1)
    panel = col * NY + layer
    owners = jnp.tile(brick_list, (1, DB // brick_list.shape[1])).reshape(-1)
    extra = (
        lax.dynamic_slice_in_dim(owners, row * TILE, TILE, 0)[:, None],
        lax.dynamic_slice_in_dim(owners, panel * TILE, TILE, 0)[None, :],
        lax.dynamic_slice_in_dim(basis, row * TILE, TILE, 0),
        lax.dynamic_slice_in_dim(basis, panel * TILE, TILE, 0),
    )
    for number in range(STEPS):
        last = number == STEPS - 1
        rows = gather_rows(own)
        out = run_step(
            number, last, place, branches, pattern, own, rows, gather_columns(own, rows[0]),
            extra if last else (),
        )
        own = out[0]
    shifted = [lax.ppermute(own, "layer", [(y, (y + hops) % NY) for y in range(NY)]) for hops in (1, 2, 3)]
    purified = join_layers(place, [own] + shifted)
    bricks = out[1].reshape(PANELS, PANELS, CB)
    bricks = lax.all_to_all(bricks, "row", 0, 0).sum(0)
    bricks = lax.all_to_all(bricks, ("col", "layer"), 0, 0, tiled=True).sum(0)
    return (purified, bricks.reshape(1, 1, 1, -1))


def solution(mesh):
    placed = (P("row", "col"), P(), P(), P(), P())
    return jax.shard_map(
        on_device,
        mesh=mesh,
        in_specs=placed,
        out_specs=(P("row", "col"), P("row", "col", "layer", None)),
        check_vma=False,
    )
```

```python
import functools

import jax
import jax.numpy as jnp
from jax import lax
from jax.experimental import pallas as pl
from jax.experimental.pallas import tpu as pltpu
from jax.sharding import PartitionSpec as P

DB = 64
STEPS = 4
TILE = 256
NZ, NX, NY = 8, 4, 4
PANELS = 16
CB = 128
BRICKS = 256
AXES = ("row", "col", "layer")


def device_number(z, core, x, y):
    return (((z % NZ) * 2 + core) * NX + x % NX) * NY + y % NY


def pairs(move):
    return [
        (device_number(z, core, x, y), device_number(*move(z, core, x, y)))
        for z in range(NZ)
        for core in range(2)
        for x in range(NX)
        for y in range(NY)
    ]


def first_leg(hops):
    return pairs(lambda z, c, x, y: (z, c, x + hops * (1 - c), y + hops * c))


def second_leg(hops):
    return pairs(lambda z, c, x, y: (z, c, x + hops * c, y + hops * (1 - c)))


def along_z(hops):
    return pairs(lambda z, c, x, y: (z + hops * (1 - 2 * c), c, x, y))


def other_core():
    return pairs(lambda z, c, x, y: (z, 1 - c, x, y))


def step_kernel(number, last, *refs):
    (place_ref, branches_ref, mask_ref, own_ref, r0, r1, r2, r3,
     own_swap, n1, n2, n3, n4, f12, f34) = refs[:15]
    refs = refs[15:]
    if last:
        row_owner_ref, col_owner_ref, row_basis_ref, col_basis_ref = refs[:4]
        out_ref, bricks_ref, column_ref, sems = refs[4:]
    else:
        out_ref, column_ref, sems = refs
    z, core, x, y = place_ref[0], place_ref[1], place_ref[2], place_ref[3]
    side = 2 * core - 1

    def put(source, offset, which_core):
        slot = ((z + offset + NZ) % NZ) * 2 + which_core
        pltpu.make_async_copy(source, column_ref.at[slot], sems.at[slot]).start()

    other = 1 - core
    put(own_ref, 0, core)
    put(own_swap, 0, other)
    for distance, near, far, at in ((1, n1, f12, 0), (2, n2, f12, 2), (3, n3, f34, 0)):
        put(near.at[0], side * distance, core)
        put(near.at[1], side * distance, other)
        put(far.at[at], -side * distance, other)
        put(far.at[at + 1], -side * distance, core)
    put(n4, 4, core)
    put(f34.at[2], 4, other)
    total = None
    for second, part in enumerate((r0, r1, r2, r3)):
        for first in range(4):
            back_x = jnp.where(core == 0, first, second)
            back_y = jnp.where(core == 0, second, first)
            k = ((x - back_x + NX) % NX) * NY + (y - back_y + NY) % NY
            pltpu.make_async_copy(own_ref, column_ref.at[k], sems.at[k]).wait()
            term = jnp.dot(part[first], column_ref[k], preferred_element_type=jnp.float32)
            total = term if total is None else total + term
    previous = own_ref[...].astype(jnp.float32)
    updated = jnp.where(branches_ref[number] == 0, total, 2.0 * previous - total)
    out_ref[...] = (updated * mask_ref[...].astype(jnp.float32)).astype(jnp.bfloat16)
    if last:
        same = row_owner_ref[...] == col_owner_ref[...]
        kept = jnp.where(same, out_ref[...].astype(jnp.float32), 0.0).astype(jnp.bfloat16)
        field = lax.dot_general(
            kept, row_basis_ref[...], (((0,), (0,)), ((), ())), preferred_element_type=jnp.float32
        )
        weights = field * col_basis_ref[...].astype(jnp.float32)
        number_of = lax.broadcasted_iota(jnp.int32, (BRICKS, TILE), 0)
        one_hot = (number_of == col_owner_ref[...]).astype(jnp.float32)
        bricks_ref[...] = jnp.dot(
            one_hot, weights, precision=lax.Precision.HIGHEST, preferred_element_type=jnp.float32
        )


def join_kernel(place_ref, t0, t1, t2, t3, out_ref):
    y = place_ref[3]
    for back, part in enumerate((t0, t1, t2, t3)):
        start = pl.multiple_of(((y - back + NY) % NY) * TILE, TILE)
        out_ref[:, pl.ds(start, TILE)] = part[...]


def join_layers(place, parts):
    vmem = pl.BlockSpec(memory_space=pltpu.VMEM)
    return pl.pallas_call(
        join_kernel,
        out_shape=jax.ShapeDtypeStruct((TILE, NY * TILE), jnp.bfloat16),
        in_specs=[pl.BlockSpec(memory_space=pltpu.SMEM)] + [vmem] * 4,
        out_specs=vmem,
        name="join_layers",
    )(place, *parts)


def run_step(number, last, place, branches, mask, own, rows, columns, extra):
    smem = pl.BlockSpec(memory_space=pltpu.SMEM)
    vmem = pl.BlockSpec(memory_space=pltpu.VMEM)
    out_shape = [jax.ShapeDtypeStruct((TILE, TILE), jnp.bfloat16)]
    if last:
        out_shape.append(jax.ShapeDtypeStruct((BRICKS, CB), jnp.float32))
    operands = (mask, own, *rows, *columns, *extra)
    return pl.pallas_call(
        functools.partial(step_kernel, number, last),
        out_shape=out_shape,
        in_specs=[smem] * 2 + [vmem] * len(operands),
        out_specs=[vmem] * len(out_shape),
        scratch_shapes=[
            pltpu.VMEM((PANELS, TILE, TILE), jnp.bfloat16),
            pltpu.SemaphoreType.DMA((PANELS,)),
        ],
        compiler_params=pltpu.CompilerParams(vmem_limit_bytes=16 << 20),
        cost_estimate=pl.CostEstimate(
            flops=2 * TILE * TILE * 4096, bytes_accessed=4 << 20, transcendentals=0
        ),
        name="square_last" if last else "square",
    )(place, branches, *operands)


def move(value, route):
    return lax.ppermute(value, AXES, route)


def gather_rows(own):
    first = jnp.stack([own] + [move(own, first_leg(hops)) for hops in (1, 2, 3)])
    return [first] + [move(first, second_leg(hops)) for hops in (1, 2, 3)]


def gather_columns(own, first):
    own_swap = move(own, other_core())
    pair = jnp.stack([own, own_swap])
    n1 = move(pair, along_z(1))
    n2 = move(pair, along_z(2))
    later, _ = lax.optimization_barrier((n2, first))
    n3 = move(later, along_z(1))
    n4 = move(later[0], along_z(2))
    f12 = move(jnp.concatenate([n1, n2]), other_core())
    f34 = move(jnp.concatenate([n3, n4[None]]), other_core())
    return [own_swap, n1, n2, n3, n4, f12, f34]


def on_device(density, pattern, branches, basis, brick_list):
    row = lax.axis_index("row")
    col = lax.axis_index("col")
    layer = lax.axis_index("layer")
    place = jnp.stack([row // 2, row % 2, col, layer]).astype(jnp.int32)
    own = lax.dynamic_slice_in_dim(density, layer * TILE, TILE, 1)
    panel = col * NY + layer
    blocks = lax.dynamic_slice(
        pattern, (row * (TILE // DB), panel * (TILE // DB)), (TILE // DB, TILE // DB)
    )
    mask = jnp.repeat(jnp.repeat(blocks.astype(jnp.bfloat16), DB, 0), DB, 1)
    owners = jnp.tile(brick_list, (1, DB // brick_list.shape[1])).reshape(-1)
    extra = (
        lax.dynamic_slice_in_dim(owners, row * TILE, TILE, 0)[:, None],
        lax.dynamic_slice_in_dim(owners, panel * TILE, TILE, 0)[None, :],
        lax.dynamic_slice_in_dim(basis, row * TILE, TILE, 0),
        lax.dynamic_slice_in_dim(basis, panel * TILE, TILE, 0),
    )
    for number in range(STEPS):
        last = number == STEPS - 1
        rows = gather_rows(own)
        out = run_step(
            number, last, place, branches, mask, own, rows, gather_columns(own, rows[0]),
            extra if last else (),
        )
        own = out[0]
    shifted = [lax.ppermute(own, "layer", [(y, (y + hops) % NY) for y in range(NY)]) for hops in (1, 2, 3)]
    purified = join_layers(place, [own] + shifted)
    bricks = out[1].reshape(PANELS, PANELS, CB)
    bricks = lax.all_to_all(bricks, "row", 0, 0).sum(0)
    bricks = lax.all_to_all(bricks, ("col", "layer"), 0, 0, tiled=True).sum(0)
    return (purified, bricks.reshape(1, 1, 1, -1))


def solution(mesh):
    placed = (P("row", "col"), P(), P(), P(), P())
    return jax.shard_map(
        on_device,
        mesh=mesh,
        in_specs=placed,
        out_specs=(P("row", "col"), P("row", "col", "layer", None)),
        check_vma=False,
    )
```

```python
import functools

import jax
import jax.numpy as jnp
from jax import lax
from jax.experimental import pallas as pl
from jax.experimental.pallas import tpu as pltpu
from jax.sharding import PartitionSpec as P

DB = 64
STEPS = 4
TILE = 256
NZ, NX, NY = 8, 4, 4
PANELS = 16
CB = 128
BRICKS = 256
AXES = ("row", "col", "layer")


def device_number(z, core, x, y):
    return (((z % NZ) * 2 + core) * NX + x % NX) * NY + y % NY


def pairs(move):
    return [
        (device_number(z, core, x, y), device_number(*move(z, core, x, y)))
        for z in range(NZ)
        for core in range(2)
        for x in range(NX)
        for y in range(NY)
    ]


def first_leg(hops):
    return pairs(lambda z, c, x, y: (z, c, x + hops * (1 - c), y + hops * c))


def second_leg(hops):
    return pairs(lambda z, c, x, y: (z, c, x + hops * c, y + hops * (1 - c)))


def along_z(hops):
    return pairs(lambda z, c, x, y: (z + hops * (1 - 2 * c), c, x, y))


def other_core():
    return pairs(lambda z, c, x, y: (z, 1 - c, x, y))


def step_kernel(number, last, *refs):
    (place_ref, branches_ref, mask_ref, own_ref, r0, r1, r2, r3,
     own_swap, n1, n2, n3, n4, f12, f34) = refs[:15]
    refs = refs[15:]
    if last:
        row_owner_ref, col_owner_ref, row_basis_ref, col_basis_ref = refs[:4]
        out_ref, bricks_ref, column_ref = refs[4:]
    else:
        out_ref, column_ref = refs
    z, core, x, y = place_ref[0], place_ref[1], place_ref[2], place_ref[3]
    side = 2 * core - 1

    def put(source, offset, which_core):
        column_ref[((z + offset + NZ) % NZ) * 2 + which_core] = source

    other = 1 - core
    put(own_ref[...], 0, core)
    put(own_swap[...], 0, other)
    for distance, near, far, at in ((1, n1, f12, 0), (2, n2, f12, 2), (3, n3, f34, 0)):
        put(near[0], side * distance, core)
        put(near[1], side * distance, other)
        put(far[at], -side * distance, other)
        put(far[at + 1], -side * distance, core)
    put(n4[...], 4, core)
    put(f34[2], 4, other)
    total = None
    for second, part in enumerate((r0, r1, r2, r3)):
        for first in range(4):
            back_x = jnp.where(core == 0, first, second)
            back_y = jnp.where(core == 0, second, first)
            k = ((x - back_x + NX) % NX) * NY + (y - back_y + NY) % NY
            term = jnp.dot(part[first], column_ref[k], preferred_element_type=jnp.float32)
            total = term if total is None else total + term
    previous = own_ref[...].astype(jnp.float32)
    updated = jnp.where(branches_ref[number] == 0, total, 2.0 * previous - total)
    out_ref[...] = (updated * mask_ref[...].astype(jnp.float32)).astype(jnp.bfloat16)
    if last:
        same = row_owner_ref[...] == col_owner_ref[...]
        kept = jnp.where(same, out_ref[...].astype(jnp.float32), 0.0).astype(jnp.bfloat16)
        field = lax.dot_general(
            kept, row_basis_ref[...], (((0,), (0,)), ((), ())), preferred_element_type=jnp.float32
        )
        weights = field * col_basis_ref[...].astype(jnp.float32)
        number_of = lax.broadcasted_iota(jnp.int32, (BRICKS, TILE), 0)
        one_hot = (number_of == col_owner_ref[...]).astype(jnp.float32)
        bricks_ref[...] = jnp.dot(
            one_hot, weights, precision=lax.Precision.HIGHEST, preferred_element_type=jnp.float32
        )


def join_kernel(place_ref, t0, t1, t2, t3, out_ref):
    y = place_ref[3]
    for back, part in enumerate((t0, t1, t2, t3)):
        start = pl.multiple_of(((y - back + NY) % NY) * TILE, TILE)
        out_ref[:, pl.ds(start, TILE)] = part[...]


def join_layers(place, parts):
    vmem = pl.BlockSpec(memory_space=pltpu.VMEM)
    return pl.pallas_call(
        join_kernel,
        out_shape=jax.ShapeDtypeStruct((TILE, NY * TILE), jnp.bfloat16),
        in_specs=[pl.BlockSpec(memory_space=pltpu.SMEM)] + [vmem] * 4,
        out_specs=vmem,
        name="join_layers",
    )(place, *parts)


def run_step(number, last, place, branches, mask, own, rows, columns, extra):
    smem = pl.BlockSpec(memory_space=pltpu.SMEM)
    vmem = pl.BlockSpec(memory_space=pltpu.VMEM)
    out_shape = [jax.ShapeDtypeStruct((TILE, TILE), jnp.bfloat16)]
    if last:
        out_shape.append(jax.ShapeDtypeStruct((BRICKS, CB), jnp.float32))
    operands = (mask, own, *rows, *columns, *extra)
    return pl.pallas_call(
        functools.partial(step_kernel, number, last),
        out_shape=out_shape,
        in_specs=[smem] * 2 + [vmem] * len(operands),
        out_specs=[vmem] * len(out_shape),
        scratch_shapes=[pltpu.VMEM((PANELS, TILE, TILE), jnp.bfloat16)],
        compiler_params=pltpu.CompilerParams(vmem_limit_bytes=16 << 20),
        cost_estimate=pl.CostEstimate(
            flops=2 * TILE * TILE * 4096, bytes_accessed=4 << 20, transcendentals=0
        ),
        name="square_last" if last else "square",
    )(place, branches, *operands)


def move(value, route):
    return lax.ppermute(value, AXES, route)


def gather_rows(own):
    first = jnp.stack([own] + [move(own, first_leg(hops)) for hops in (1, 2, 3)])
    return [first] + [move(first, second_leg(hops)) for hops in (1, 2, 3)]


def gather_columns(own, first):
    own_swap = move(own, other_core())
    pair = jnp.stack([own, own_swap])
    n1 = move(pair, along_z(1))
    n2 = move(pair, along_z(2))
    later, _ = lax.optimization_barrier((n2, first))
    n3 = move(later, along_z(1))
    n4 = move(later[0], along_z(2))
    f12 = move(jnp.concatenate([n1, n2]), other_core())
    f34 = move(jnp.concatenate([n3, n4[None]]), other_core())
    return [own_swap, n1, n2, n3, n4, f12, f34]


def on_device(density, pattern, branches, basis, brick_list):
    row = lax.axis_index("row")
    col = lax.axis_index("col")
    layer = lax.axis_index("layer")
    place = jnp.stack([row // 2, row % 2, col, layer]).astype(jnp.int32)
    own = lax.dynamic_slice_in_dim(density, layer * TILE, TILE, 1)
    panel = col * NY + layer
    blocks = lax.dynamic_slice(
        pattern, (row * (TILE // DB), panel * (TILE // DB)), (TILE // DB, TILE // DB)
    )
    mask = jnp.repeat(jnp.repeat(blocks.astype(jnp.bfloat16), DB, 0), DB, 1)
    owners = jnp.tile(brick_list, (1, DB // brick_list.shape[1])).reshape(-1)
    extra = (
        lax.dynamic_slice_in_dim(owners, row * TILE, TILE, 0)[:, None],
        lax.dynamic_slice_in_dim(owners, panel * TILE, TILE, 0)[None, :],
        lax.dynamic_slice_in_dim(basis, row * TILE, TILE, 0),
        lax.dynamic_slice_in_dim(basis, panel * TILE, TILE, 0),
    )
    for number in range(STEPS):
        last = number == STEPS - 1
        rows = gather_rows(own)
        out = run_step(
            number, last, place, branches, mask, own, rows, gather_columns(own, rows[0]),
            extra if last else (),
        )
        own = out[0]
    shifted = [lax.ppermute(own, "layer", [(y, (y + hops) % NY) for y in range(NY)]) for hops in (1, 2, 3)]
    purified = join_layers(place, [own] + shifted)
    bricks = out[1].reshape(PANELS, PANELS, CB)
    bricks = lax.all_to_all(bricks, "row", 0, 0).sum(0)
    bricks = lax.all_to_all(bricks, ("col", "layer"), 0, 0, tiled=True).sum(0)
    return (purified, bricks.reshape(1, 1, 1, -1))


def solution(mesh):
    placed = (P("row", "col"), P(), P(), P(), P())
    return jax.shard_map(
        on_device,
        mesh=mesh,
        in_specs=placed,
        out_specs=(P("row", "col"), P("row", "col", "layer", None)),
        check_vma=False,
    )
```

```python
import functools

import jax
import jax.numpy as jnp
from jax import lax
from jax.experimental import pallas as pl
from jax.experimental.pallas import tpu as pltpu
from jax.sharding import PartitionSpec as P

DB = 64
STEPS = 4
TILE = 256
NZ, NX, NY = 8, 4, 4
PANELS = 16
CB = 128
BRICKS = 256
AFTER_ROWS = 20 * 10**9
AXES = ("row", "col", "layer")


def device_number(z, core, x, y):
    return (((z % NZ) * 2 + core) * NX + x % NX) * NY + y % NY


def pairs(move):
    return [
        (device_number(z, core, x, y), device_number(*move(z, core, x, y)))
        for z in range(NZ)
        for core in range(2)
        for x in range(NX)
        for y in range(NY)
    ]


def first_leg(hops):
    return pairs(lambda z, c, x, y: (z, c, x + hops * (1 - c), y + hops * c))


def second_leg(hops):
    return pairs(lambda z, c, x, y: (z, c, x + hops * c, y + hops * (1 - c)))


def along_z(hops):
    return pairs(lambda z, c, x, y: (z + hops * (1 - 2 * c), c, x, y))


def other_core():
    return pairs(lambda z, c, x, y: (z, 1 - c, x, y))


def step_kernel(number, last, *refs):
    (place_ref, branches_ref, mask_ref, own_ref, r0, r1, r2, r3,
     own_swap, n1, n2, n3, n4, f12, f34, _) = refs[:16]
    refs = refs[16:]
    if last:
        row_owner_ref, col_owner_ref, row_basis_ref, col_basis_ref = refs[:4]
        out_ref, bricks_ref, column_ref = refs[4:]
    else:
        out_ref, column_ref = refs
    z, core, x, y = place_ref[0], place_ref[1], place_ref[2], place_ref[3]
    side = 2 * core - 1

    def put(source, offset, which_core):
        column_ref[((z + offset + NZ) % NZ) * 2 + which_core] = source

    other = 1 - core
    put(own_ref[...], 0, core)
    put(own_swap[...], 0, other)
    for distance, near, far, at in ((1, n1, f12, 0), (2, n2, f12, 2), (3, n3, f34, 0)):
        put(near[0], side * distance, core)
        put(near[1], side * distance, other)
        put(far[at], -side * distance, other)
        put(far[at + 1], -side * distance, core)
    put(n4[...], 4, core)
    put(f34[2], 4, other)
    total = None
    for second, part in enumerate((r0, r1, r2, r3)):
        for first in range(4):
            back_x = jnp.where(core == 0, first, second)
            back_y = jnp.where(core == 0, second, first)
            k = ((x - back_x + NX) % NX) * NY + (y - back_y + NY) % NY
            term = jnp.dot(part[first], column_ref[k], preferred_element_type=jnp.float32)
            total = term if total is None else total + term
    previous = own_ref[...].astype(jnp.float32)
    updated = jnp.where(branches_ref[number] == 0, total, 2.0 * previous - total)
    out_ref[...] = (updated * mask_ref[...].astype(jnp.float32)).astype(jnp.bfloat16)
    if last:
        same = row_owner_ref[...] == col_owner_ref[...]
        kept = jnp.where(same, out_ref[...].astype(jnp.float32), 0.0).astype(jnp.bfloat16)
        field = lax.dot_general(
            kept, row_basis_ref[...], (((0,), (0,)), ((), ())), preferred_element_type=jnp.float32
        )
        weights = field * col_basis_ref[...].astype(jnp.float32)
        number_of = lax.broadcasted_iota(jnp.int32, (BRICKS, TILE), 0)
        one_hot = (number_of == col_owner_ref[...]).astype(jnp.float32)
        bricks_ref[...] = jnp.dot(
            one_hot, weights, precision=lax.Precision.HIGHEST, preferred_element_type=jnp.float32
        )


def arrived_kernel(*refs):
    refs[-1][...] = jnp.zeros_like(refs[-1])


def arrived(parts):
    return pl.pallas_call(
        arrived_kernel,
        out_shape=jax.ShapeDtypeStruct((8, 128), jnp.float32),
        in_specs=[pl.BlockSpec(memory_space=pl.ANY)] * len(parts),
        out_specs=pl.BlockSpec(memory_space=pltpu.VMEM),
        cost_estimate=pl.CostEstimate(flops=AFTER_ROWS, bytes_accessed=4096, transcendentals=0),
        name="arrived",
    )(*parts)


def join_kernel(place_ref, t0, t1, t2, t3, out_ref):
    y = place_ref[3]
    for back, part in enumerate((t0, t1, t2, t3)):
        start = pl.multiple_of(((y - back + NY) % NY) * TILE, TILE)
        out_ref[:, pl.ds(start, TILE)] = part[...]


def join_layers(place, parts):
    vmem = pl.BlockSpec(memory_space=pltpu.VMEM)
    return pl.pallas_call(
        join_kernel,
        out_shape=jax.ShapeDtypeStruct((TILE, NY * TILE), jnp.bfloat16),
        in_specs=[pl.BlockSpec(memory_space=pltpu.SMEM)] + [vmem] * 4,
        out_specs=vmem,
        name="join_layers",
    )(place, *parts)


def run_step(number, last, place, branches, mask, own, rows, columns, extra):
    smem = pl.BlockSpec(memory_space=pltpu.SMEM)
    vmem = pl.BlockSpec(memory_space=pltpu.VMEM)
    out_shape = [jax.ShapeDtypeStruct((TILE, TILE), jnp.bfloat16)]
    if last:
        out_shape.append(jax.ShapeDtypeStruct((BRICKS, CB), jnp.float32))
    operands = (mask, own, *rows, *columns, arrived(rows[1:]), *extra)
    return pl.pallas_call(
        functools.partial(step_kernel, number, last),
        out_shape=out_shape,
        in_specs=[smem] * 2 + [vmem] * len(operands),
        out_specs=[vmem] * len(out_shape),
        scratch_shapes=[pltpu.VMEM((PANELS, TILE, TILE), jnp.bfloat16)],
        compiler_params=pltpu.CompilerParams(vmem_limit_bytes=16 << 20),
        cost_estimate=pl.CostEstimate(
            flops=2 * TILE * TILE * 4096, bytes_accessed=4 << 20, transcendentals=0
        ),
        name="square_last" if last else "square",
    )(place, branches, *operands)


def move(value, route):
    return lax.ppermute(value, AXES, route)


def gather_rows(own):
    first = jnp.stack([own] + [move(own, first_leg(hops)) for hops in (1, 2, 3)])
    return [first] + [move(first, second_leg(hops)) for hops in (1, 2, 3)]


def gather_columns(own, first):
    own_swap = move(own, other_core())
    pair = jnp.stack([own, own_swap])
    n1 = move(pair, along_z(1))
    n2 = move(pair, along_z(2))
    later, _ = lax.optimization_barrier((n2, first))
    n3 = move(later, along_z(1))
    n4 = move(later[0], along_z(2))
    f12 = move(jnp.concatenate([n1, n2]), other_core())
    f34 = move(jnp.concatenate([n3, n4[None]]), other_core())
    return [own_swap, n1, n2, n3, n4, f12, f34]


def on_device(density, pattern, branches, basis, brick_list):
    row = lax.axis_index("row")
    col = lax.axis_index("col")
    layer = lax.axis_index("layer")
    place = jnp.stack([row // 2, row % 2, col, layer]).astype(jnp.int32)
    own = lax.dynamic_slice_in_dim(density, layer * TILE, TILE, 1)
    panel = col * NY + layer
    blocks = lax.dynamic_slice(
        pattern, (row * (TILE // DB), panel * (TILE // DB)), (TILE // DB, TILE // DB)
    )
    mask = jnp.repeat(jnp.repeat(blocks.astype(jnp.bfloat16), DB, 0), DB, 1)
    owners = jnp.tile(brick_list, (1, DB // brick_list.shape[1])).reshape(-1)
    extra = (
        lax.dynamic_slice_in_dim(owners, row * TILE, TILE, 0)[:, None],
        lax.dynamic_slice_in_dim(owners, panel * TILE, TILE, 0)[None, :],
        lax.dynamic_slice_in_dim(basis, row * TILE, TILE, 0),
        lax.dynamic_slice_in_dim(basis, panel * TILE, TILE, 0),
    )
    for number in range(STEPS):
        last = number == STEPS - 1
        rows = gather_rows(own)
        out = run_step(
            number, last, place, branches, mask, own, rows, gather_columns(own, rows[0]),
            extra if last else (),
        )
        own = out[0]
    shifted = [lax.ppermute(own, "layer", [(y, (y + hops) % NY) for y in range(NY)]) for hops in (1, 2, 3)]
    purified = join_layers(place, [own] + shifted)
    bricks = out[1].reshape(PANELS, PANELS, CB)
    bricks = lax.all_to_all(bricks, "row", 0, 0).sum(0)
    bricks = lax.all_to_all(bricks, ("col", "layer"), 0, 0, tiled=True).sum(0)
    return (purified, bricks.reshape(1, 1, 1, -1))


def solution(mesh):
    placed = (P("row", "col"), P(), P(), P(), P())
    return jax.shard_map(
        on_device,
        mesh=mesh,
        in_specs=placed,
        out_specs=(P("row", "col"), P("row", "col", "layer", None)),
        check_vma=False,
    )
```

```python
import functools

import jax
import jax.numpy as jnp
from jax import lax
from jax.experimental import pallas as pl
from jax.experimental.pallas import tpu as pltpu
from jax.sharding import PartitionSpec as P

DB = 64
STEPS = 4
TILE = 256
NZ, NX, NY = 8, 4, 4
PANELS = 16
CB = 128
BRICKS = 256
AFTER_ROWS = 20 * 10**9
AXES = ("row", "col", "layer")


def device_number(z, core, x, y):
    return (((z % NZ) * 2 + core) * NX + x % NX) * NY + y % NY


def pairs(move):
    return [
        (device_number(z, core, x, y), device_number(*move(z, core, x, y)))
        for z in range(NZ)
        for core in range(2)
        for x in range(NX)
        for y in range(NY)
    ]


def first_leg(hops):
    return pairs(lambda z, c, x, y: (z, c, x + hops * (1 - c), y + hops * c))


def second_leg(hops):
    return pairs(lambda z, c, x, y: (z, c, x + hops * c, y + hops * (1 - c)))


def along_z(hops):
    return pairs(lambda z, c, x, y: (z + hops * (1 - 2 * c), c, x, y))


def other_core():
    return pairs(lambda z, c, x, y: (z, 1 - c, x, y))


def step_kernel(number, last, *refs):
    (place_ref, branches_ref, mask_ref, own_ref, r0, r1, r2, r3,
     own_swap, n1, n2, n3, n4, f12, f34, _) = refs[:16]
    refs = refs[16:]
    if last:
        row_owner_ref, col_owner_ref, row_basis_ref, col_basis_ref = refs[:4]
        out_ref, bricks_ref, column_ref = refs[4:]
    else:
        out_ref, column_ref = refs
    z, core, x, y = place_ref[0], place_ref[1], place_ref[2], place_ref[3]
    side = 2 * core - 1

    def put(source, offset, which_core):
        column_ref[((z + offset + NZ) % NZ) * 2 + which_core] = source

    other = 1 - core
    put(own_ref[...], 0, core)
    put(own_swap[...], 0, other)
    for distance, near, far, at in ((1, n1, f12, 0), (2, n2, f12, 2), (3, n3, f34, 0)):
        put(near[0], side * distance, core)
        put(near[1], side * distance, other)
        put(far[at], -side * distance, other)
        put(far[at + 1], -side * distance, core)
    put(n4[...], 4, core)
    put(f34[2], 4, other)
    total = None
    for second, part in enumerate((r0, r1, r2, r3)):
        for first in range(4):
            back_x = jnp.where(core == 0, first, second)
            back_y = jnp.where(core == 0, second, first)
            k = ((x - back_x + NX) % NX) * NY + (y - back_y + NY) % NY
            term = jnp.dot(part[first], column_ref[k], preferred_element_type=jnp.float32)
            total = term if total is None else total + term
    previous = own_ref[...].astype(jnp.float32)
    updated = jnp.where(branches_ref[number] == 0, total, 2.0 * previous - total)
    out_ref[...] = (updated * mask_ref[...].astype(jnp.float32)).astype(jnp.bfloat16)
    if last:
        same = row_owner_ref[...] == col_owner_ref[...]
        kept = jnp.where(same, out_ref[...].astype(jnp.float32), 0.0).astype(jnp.bfloat16)
        field = lax.dot_general(
            kept, row_basis_ref[...], (((0,), (0,)), ((), ())), preferred_element_type=jnp.float32
        )
        weights = field * col_basis_ref[...].astype(jnp.float32)
        number_of = lax.broadcasted_iota(jnp.int32, (BRICKS, TILE), 0)
        one_hot = (number_of == col_owner_ref[...]).astype(jnp.float32)
        bricks_ref[...] = jnp.dot(
            one_hot, weights, precision=lax.Precision.HIGHEST, preferred_element_type=jnp.float32
        )


def arrived_kernel(*refs):
    refs[-1][...] = jnp.zeros_like(refs[-1])


def arrived(parts):
    return pl.pallas_call(
        arrived_kernel,
        out_shape=jax.ShapeDtypeStruct((8, 128), jnp.float32),
        in_specs=[pl.BlockSpec(memory_space=pltpu.VMEM)] * len(parts),
        out_specs=pl.BlockSpec(memory_space=pltpu.VMEM),
        cost_estimate=pl.CostEstimate(flops=AFTER_ROWS, bytes_accessed=4096, transcendentals=0),
        name="arrived",
    )(*parts)


def join_kernel(place_ref, t0, t1, t2, t3, out_ref):
    y = place_ref[3]
    for back, part in enumerate((t0, t1, t2, t3)):
        start = pl.multiple_of(((y - back + NY) % NY) * TILE, TILE)
        out_ref[:, pl.ds(start, TILE)] = part[...]


def join_layers(place, parts):
    vmem = pl.BlockSpec(memory_space=pltpu.VMEM)
    return pl.pallas_call(
        join_kernel,
        out_shape=jax.ShapeDtypeStruct((TILE, NY * TILE), jnp.bfloat16),
        in_specs=[pl.BlockSpec(memory_space=pltpu.SMEM)] + [vmem] * 4,
        out_specs=vmem,
        name="join_layers",
    )(place, *parts)


def run_step(number, last, place, branches, mask, own, rows, columns, extra):
    smem = pl.BlockSpec(memory_space=pltpu.SMEM)
    vmem = pl.BlockSpec(memory_space=pltpu.VMEM)
    out_shape = [jax.ShapeDtypeStruct((TILE, TILE), jnp.bfloat16)]
    if last:
        out_shape.append(jax.ShapeDtypeStruct((BRICKS, CB), jnp.float32))
    operands = (mask, own, *rows, *columns, arrived(rows[1:]), *extra)
    return pl.pallas_call(
        functools.partial(step_kernel, number, last),
        out_shape=out_shape,
        in_specs=[smem] * 2 + [vmem] * len(operands),
        out_specs=[vmem] * len(out_shape),
        scratch_shapes=[pltpu.VMEM((PANELS, TILE, TILE), jnp.bfloat16)],
        compiler_params=pltpu.CompilerParams(vmem_limit_bytes=16 << 20),
        cost_estimate=pl.CostEstimate(
            flops=2 * TILE * TILE * 4096, bytes_accessed=4 << 20, transcendentals=0
        ),
        name="square_last" if last else "square",
    )(place, branches, *operands)


def move(value, route):
    return lax.ppermute(value, AXES, route)


def gather_rows(own):
    first = jnp.stack([own] + [move(own, first_leg(hops)) for hops in (1, 2, 3)])
    return [first] + [move(first, second_leg(hops)) for hops in (1, 2, 3)]


def gather_columns(own, first):
    own_swap = move(own, other_core())
    pair = jnp.stack([own, own_swap])
    n1 = move(pair, along_z(1))
    n2 = move(pair, along_z(2))
    later, _, _ = lax.optimization_barrier((n2, n1, first))
    n3 = move(later, along_z(1))
    n4 = move(later[0], along_z(2))
    f12 = move(jnp.concatenate([n1, n2]), other_core())
    f34 = move(jnp.concatenate([n3, n4[None]]), other_core())
    return [own_swap, n1, n2, n3, n4, f12, f34]


def on_device(density, pattern, branches, basis, brick_list):
    row = lax.axis_index("row")
    col = lax.axis_index("col")
    layer = lax.axis_index("layer")
    place = jnp.stack([row // 2, row % 2, col, layer]).astype(jnp.int32)
    own = lax.dynamic_slice_in_dim(density, layer * TILE, TILE, 1)
    panel = col * NY + layer
    blocks = lax.dynamic_slice(
        pattern, (row * (TILE // DB), panel * (TILE // DB)), (TILE // DB, TILE // DB)
    )
    mask = jnp.repeat(jnp.repeat(blocks.astype(jnp.bfloat16), DB, 0), DB, 1)
    owners = jnp.tile(brick_list, (1, DB // brick_list.shape[1])).reshape(-1)
    extra = (
        lax.dynamic_slice_in_dim(owners, row * TILE, TILE, 0)[:, None],
        lax.dynamic_slice_in_dim(owners, panel * TILE, TILE, 0)[None, :],
        lax.dynamic_slice_in_dim(basis, row * TILE, TILE, 0),
        lax.dynamic_slice_in_dim(basis, panel * TILE, TILE, 0),
    )
    for number in range(STEPS):
        last = number == STEPS - 1
        rows = gather_rows(own)
        out = run_step(
            number, last, place, branches, mask, own, rows, gather_columns(own, rows[0]),
            extra if last else (),
        )
        own = out[0]
    shifted = [lax.ppermute(own, "layer", [(y, (y + hops) % NY) for y in range(NY)]) for hops in (1, 2, 3)]
    purified = join_layers(place, [own] + shifted)
    bricks = out[1].reshape(PANELS, PANELS, CB)
    bricks = lax.all_to_all(bricks, "row", 0, 0).sum(0)
    bricks = lax.all_to_all(bricks, ("col", "layer"), 0, 0, tiled=True).sum(0)
    return (purified, bricks.reshape(1, 1, 1, -1))


def solution(mesh):
    placed = (P("row", "col"), P(), P(), P(), P())
    return jax.shard_map(
        on_device,
        mesh=mesh,
        in_specs=placed,
        out_specs=(P("row", "col"), P("row", "col", "layer", None)),
        check_vma=False,
    )
```

```python
import functools

import jax
import jax.numpy as jnp
from jax import lax
from jax.experimental import pallas as pl
from jax.experimental.pallas import tpu as pltpu
from jax.sharding import PartitionSpec as P

DB = 64
STEPS = 4
TILE = 256
NZ, NX, NY = 8, 4, 4
PANELS = 16
CB = 128
BRICKS = 256
PART_FLOPS = 3 * 10**9
AXES = ("row", "col", "layer")


def device_number(z, core, x, y):
    return (((z % NZ) * 2 + core) * NX + x % NX) * NY + y % NY


def pairs(move):
    return [
        (device_number(z, core, x, y), device_number(*move(z, core, x, y)))
        for z in range(NZ)
        for core in range(2)
        for x in range(NX)
        for y in range(NY)
    ]


def first_leg(hops):
    return pairs(lambda z, c, x, y: (z, c, x + hops * (1 - c), y + hops * c))


def second_leg(hops):
    return pairs(lambda z, c, x, y: (z, c, x + hops * c, y + hops * (1 - c)))


def along_z(hops):
    return pairs(lambda z, c, x, y: (z + hops * (1 - 2 * c), c, x, y))


def other_core():
    return pairs(lambda z, c, x, y: (z, 1 - c, x, y))


def part_kernel(place_ref, own_ref, r0, r1, r2, r3, own_swap, n1, n2, n34, f12, total_ref,
                late_ref, column_ref):
    z, core, x, y = place_ref[0], place_ref[1], place_ref[2], place_ref[3]
    side = 2 * core - 1
    other = 1 - core

    def slot(offset, which_core):
        return ((z + offset + NZ) % NZ) * 2 + which_core

    column_ref[slot(0, core)] = own_ref[...]
    column_ref[slot(0, other)] = own_swap[...]
    for distance, near in ((1, n1), (2, n2), (3, n34)):
        column_ref[slot(side * distance, core)] = near[0]
        column_ref[slot(side * distance, other)] = near[1]
    for distance, at in ((1, 0), (2, 2)):
        column_ref[slot(-side * distance, other)] = f12[at]
        column_ref[slot(-side * distance, core)] = f12[at + 1]
    column_ref[slot(4, core)] = n34[2]
    parts = (r0, r1, r2, r3)
    late = (slot(-side * 3, other), slot(-side * 3, core), slot(4, other))
    for at, k in enumerate(late):
        column_ref[k] = jnp.zeros((TILE, TILE), jnp.bfloat16)
        back_x = (x - k // NY + NX) % NX
        back_y = (y - k % NY + NY) % NY
        first = jnp.where(core == 0, back_x, back_y)
        second = jnp.where(core == 0, back_y, back_x)
        for number, part in enumerate(parts):
            @pl.when(second == number)
            def _():
                late_ref[at] = part[first]
    total = None
    for second, part in enumerate(parts):
        for first in range(4):
            back_x = jnp.where(core == 0, first, second)
            back_y = jnp.where(core == 0, second, first)
            k = ((x - back_x + NX) % NX) * NY + (y - back_y + NY) % NY
            term = jnp.dot(part[first], column_ref[k], preferred_element_type=jnp.float32)
            total = term if total is None else total + term
    total_ref[...] = total


def finish_kernel(number, last, *refs):
    branches_ref, mask_ref, own_ref, total_ref, late_ref, f34 = refs[:6]
    refs = refs[6:]
    if last:
        row_owner_ref, col_owner_ref, row_basis_ref, col_basis_ref, out_ref, bricks_ref = refs
    else:
        (out_ref,) = refs
    total = total_ref[...]
    for at in range(3):
        total += jnp.dot(late_ref[at], f34[at], preferred_element_type=jnp.float32)
    previous = own_ref[...].astype(jnp.float32)
    updated = jnp.where(branches_ref[number] == 0, total, 2.0 * previous - total)
    out_ref[...] = (updated * mask_ref[...].astype(jnp.float32)).astype(jnp.bfloat16)
    if last:
        same = row_owner_ref[...] == col_owner_ref[...]
        kept = jnp.where(same, out_ref[...].astype(jnp.float32), 0.0).astype(jnp.bfloat16)
        field = lax.dot_general(
            kept, row_basis_ref[...], (((0,), (0,)), ((), ())), preferred_element_type=jnp.float32
        )
        weights = field * col_basis_ref[...].astype(jnp.float32)
        number_of = lax.broadcasted_iota(jnp.int32, (BRICKS, TILE), 0)
        one_hot = (number_of == col_owner_ref[...]).astype(jnp.float32)
        bricks_ref[...] = jnp.dot(
            one_hot, weights, precision=lax.Precision.HIGHEST, preferred_element_type=jnp.float32
        )


def join_kernel(place_ref, t0, t1, t2, t3, out_ref):
    y = place_ref[3]
    for back, part in enumerate((t0, t1, t2, t3)):
        start = pl.multiple_of(((y - back + NY) % NY) * TILE, TILE)
        out_ref[:, pl.ds(start, TILE)] = part[...]


def join_layers(place, parts):
    vmem = pl.BlockSpec(memory_space=pltpu.VMEM)
    return pl.pallas_call(
        join_kernel,
        out_shape=jax.ShapeDtypeStruct((TILE, NY * TILE), jnp.bfloat16),
        in_specs=[pl.BlockSpec(memory_space=pltpu.SMEM)] + [vmem] * 4,
        out_specs=vmem,
        name="join_layers",
    )(place, *parts)


def run_step(number, last, place, branches, mask, own, rows, columns, extra):
    smem = pl.BlockSpec(memory_space=pltpu.SMEM)
    vmem = pl.BlockSpec(memory_space=pltpu.VMEM)
    *early, f34 = columns
    operands = (own, *rows, *early)
    total, late = pl.pallas_call(
        part_kernel,
        out_shape=[
            jax.ShapeDtypeStruct((TILE, TILE), jnp.float32),
            jax.ShapeDtypeStruct((3, TILE, TILE), jnp.bfloat16),
        ],
        in_specs=[smem] + [vmem] * len(operands),
        out_specs=[vmem] * 2,
        scratch_shapes=[pltpu.VMEM((PANELS, TILE, TILE), jnp.bfloat16)],
        compiler_params=pltpu.CompilerParams(vmem_limit_bytes=16 << 20),
        cost_estimate=pl.CostEstimate(flops=PART_FLOPS, bytes_accessed=4 << 20, transcendentals=0),
        name="square_part",
    )(place, *operands)
    out_shape = [jax.ShapeDtypeStruct((TILE, TILE), jnp.bfloat16)]
    if last:
        out_shape.append(jax.ShapeDtypeStruct((BRICKS, CB), jnp.float32))
    operands = (mask, own, total, late, f34, *extra)
    return pl.pallas_call(
        functools.partial(finish_kernel, number, last),
        out_shape=out_shape,
        in_specs=[smem] + [vmem] * len(operands),
        out_specs=[vmem] * len(out_shape),
        compiler_params=pltpu.CompilerParams(vmem_limit_bytes=16 << 20),
        cost_estimate=pl.CostEstimate(
            flops=6 * TILE**3, bytes_accessed=1 << 20, transcendentals=0
        ),
        name="square_last" if last else "square",
    )(branches, *operands)


def move(value, route):
    return lax.ppermute(value, AXES, route)


def gather_rows(own):
    first = jnp.stack([own] + [move(own, first_leg(hops)) for hops in (1, 2, 3)])
    return [first] + [move(first, second_leg(hops)) for hops in (1, 2, 3)]


def gather_columns(own, first):
    own_swap = move(own, other_core())
    pair = jnp.stack([own, own_swap])
    n1 = move(pair, along_z(1))
    n2 = move(pair, along_z(2))
    ahead, _ = lax.optimization_barrier((jnp.concatenate([n1, n2[:1]]), first))
    n34 = move(ahead, along_z(2))
    f12 = move(jnp.concatenate([n1, n2]), other_core())
    f34 = move(n34, other_core())
    return [own_swap, n1, n2, n34, f12, f34]


def on_device(density, pattern, branches, basis, brick_list):
    row = lax.axis_index("row")
    col = lax.axis_index("col")
    layer = lax.axis_index("layer")
    place = jnp.stack([row // 2, row % 2, col, layer]).astype(jnp.int32)
    own = lax.dynamic_slice_in_dim(density, layer * TILE, TILE, 1)
    panel = col * NY + layer
    blocks = lax.dynamic_slice(
        pattern, (row * (TILE // DB), panel * (TILE // DB)), (TILE // DB, TILE // DB)
    )
    mask = jnp.repeat(jnp.repeat(blocks.astype(jnp.bfloat16), DB, 0), DB, 1)
    owners = jnp.tile(brick_list, (1, DB // brick_list.shape[1])).reshape(-1)
    extra = (
        lax.dynamic_slice_in_dim(owners, row * TILE, TILE, 0)[:, None],
        lax.dynamic_slice_in_dim(owners, panel * TILE, TILE, 0)[None, :],
        lax.dynamic_slice_in_dim(basis, row * TILE, TILE, 0),
        lax.dynamic_slice_in_dim(basis, panel * TILE, TILE, 0),
    )
    for number in range(STEPS):
        last = number == STEPS - 1
        rows = gather_rows(own)
        out = run_step(
            number, last, place, branches, mask, own, rows, gather_columns(own, rows[0]),
            extra if last else (),
        )
        own = out[0]
    shifted = [lax.ppermute(own, "layer", [(y, (y + hops) % NY) for y in range(NY)]) for hops in (1, 2, 3)]
    purified = join_layers(place, [own] + shifted)
    bricks = out[1].reshape(PANELS, PANELS, CB)
    bricks = lax.all_to_all(bricks, "row", 0, 0).sum(0)
    bricks = lax.all_to_all(bricks, ("col", "layer"), 0, 0, tiled=True).sum(0)
    return (purified, bricks.reshape(1, 1, 1, -1))


def solution(mesh):
    placed = (P("row", "col"), P(), P(), P(), P())
    return jax.shard_map(
        on_device,
        mesh=mesh,
        in_specs=placed,
        out_specs=(P("row", "col"), P("row", "col", "layer", None)),
        check_vma=False,
    )
```

```python
import functools

import jax
import jax.numpy as jnp
from jax import lax
from jax.experimental import pallas as pl
from jax.experimental.pallas import tpu as pltpu
from jax.sharding import PartitionSpec as P

DB = 64
STEPS = 4
TILE = 256
NZ, NX, NY = 8, 4, 4
PANELS = 16
CB = 128
BRICKS = 256
PART_FLOPS = 3 * 10**9
AXES = ("row", "col", "layer")


def device_number(z, core, x, y):
    return (((z % NZ) * 2 + core) * NX + x % NX) * NY + y % NY


def pairs(move):
    return [
        (device_number(z, core, x, y), device_number(*move(z, core, x, y)))
        for z in range(NZ)
        for core in range(2)
        for x in range(NX)
        for y in range(NY)
    ]


def first_leg(hops):
    return pairs(lambda z, c, x, y: (z, c, x + hops * (1 - c), y + hops * c))


def second_leg(hops):
    return pairs(lambda z, c, x, y: (z, c, x + hops * c, y + hops * (1 - c)))


def along_z(hops):
    return pairs(lambda z, c, x, y: (z + hops * (1 - 2 * c), c, x, y))


def other_core():
    return pairs(lambda z, c, x, y: (z, 1 - c, x, y))


def part_kernel(place_ref, own_ref, r0, r1, r2, r3, own_swap, n1, n2, n3, n4, f12, total_ref,
                late_ref, column_ref):
    z, core, x, y = place_ref[0], place_ref[1], place_ref[2], place_ref[3]
    side = 2 * core - 1
    other = 1 - core

    def slot(offset, which_core):
        return ((z + offset + NZ) % NZ) * 2 + which_core

    column_ref[slot(0, core)] = own_ref[...]
    column_ref[slot(0, other)] = own_swap[...]
    for distance, near in ((1, n1), (2, n2), (3, n3)):
        column_ref[slot(side * distance, core)] = near[0]
        column_ref[slot(side * distance, other)] = near[1]
    for distance, at in ((1, 0), (2, 2)):
        column_ref[slot(-side * distance, other)] = f12[at]
        column_ref[slot(-side * distance, core)] = f12[at + 1]
    column_ref[slot(4, core)] = n4[...]
    parts = (r0, r1, r2, r3)
    late = (slot(-side * 3, other), slot(-side * 3, core), slot(4, other))
    for at, k in enumerate(late):
        column_ref[k] = jnp.zeros((TILE, TILE), jnp.bfloat16)
        back_x = (x - k // NY + NX) % NX
        back_y = (y - k % NY + NY) % NY
        first = jnp.where(core == 0, back_x, back_y)
        second = jnp.where(core == 0, back_y, back_x)
        for number, part in enumerate(parts):
            @pl.when(second == number)
            def _():
                late_ref[at] = part[first]
    total = None
    for second, part in enumerate(parts):
        for first in range(4):
            back_x = jnp.where(core == 0, first, second)
            back_y = jnp.where(core == 0, second, first)
            k = ((x - back_x + NX) % NX) * NY + (y - back_y + NY) % NY
            term = jnp.dot(part[first], column_ref[k], preferred_element_type=jnp.float32)
            total = term if total is None else total + term
    total_ref[...] = total


def finish_kernel(number, last, *refs):
    branches_ref, mask_ref, own_ref, total_ref, late_ref, f34 = refs[:6]
    refs = refs[6:]
    if last:
        row_owner_ref, col_owner_ref, row_basis_ref, col_basis_ref, out_ref, bricks_ref = refs
    else:
        (out_ref,) = refs
    total = total_ref[...]
    for at in range(3):
        total += jnp.dot(late_ref[at], f34[at], preferred_element_type=jnp.float32)
    previous = own_ref[...].astype(jnp.float32)
    updated = jnp.where(branches_ref[number] == 0, total, 2.0 * previous - total)
    out_ref[...] = (updated * mask_ref[...].astype(jnp.float32)).astype(jnp.bfloat16)
    if last:
        same = row_owner_ref[...] == col_owner_ref[...]
        kept = jnp.where(same, out_ref[...].astype(jnp.float32), 0.0).astype(jnp.bfloat16)
        field = lax.dot_general(
            kept, row_basis_ref[...], (((0,), (0,)), ((), ())), preferred_element_type=jnp.float32
        )
        weights = field * col_basis_ref[...].astype(jnp.float32)
        number_of = lax.broadcasted_iota(jnp.int32, (BRICKS, TILE), 0)
        one_hot = (number_of == col_owner_ref[...]).astype(jnp.float32)
        bricks_ref[...] = jnp.dot(
            one_hot, weights, precision=lax.Precision.HIGHEST, preferred_element_type=jnp.float32
        )


def join_kernel(place_ref, t0, t1, t2, t3, out_ref):
    y = place_ref[3]
    for back, part in enumerate((t0, t1, t2, t3)):
        start = pl.multiple_of(((y - back + NY) % NY) * TILE, TILE)
        out_ref[:, pl.ds(start, TILE)] = part[...]


def join_layers(place, parts):
    vmem = pl.BlockSpec(memory_space=pltpu.VMEM)
    return pl.pallas_call(
        join_kernel,
        out_shape=jax.ShapeDtypeStruct((TILE, NY * TILE), jnp.bfloat16),
        in_specs=[pl.BlockSpec(memory_space=pltpu.SMEM)] + [vmem] * 4,
        out_specs=vmem,
        name="join_layers",
    )(place, *parts)


def run_step(number, last, place, branches, mask, own, rows, columns, extra):
    smem = pl.BlockSpec(memory_space=pltpu.SMEM)
    vmem = pl.BlockSpec(memory_space=pltpu.VMEM)
    *early, f34 = columns
    operands = (own, *rows, *early)
    total, late = pl.pallas_call(
        part_kernel,
        out_shape=[
            jax.ShapeDtypeStruct((TILE, TILE), jnp.float32),
            jax.ShapeDtypeStruct((3, TILE, TILE), jnp.bfloat16),
        ],
        in_specs=[smem] + [vmem] * len(operands),
        out_specs=[vmem] * 2,
        scratch_shapes=[pltpu.VMEM((PANELS, TILE, TILE), jnp.bfloat16)],
        compiler_params=pltpu.CompilerParams(vmem_limit_bytes=16 << 20),
        cost_estimate=pl.CostEstimate(flops=PART_FLOPS, bytes_accessed=4 << 20, transcendentals=0),
        name="square_part",
    )(place, *operands)
    out_shape = [jax.ShapeDtypeStruct((TILE, TILE), jnp.bfloat16)]
    if last:
        out_shape.append(jax.ShapeDtypeStruct((BRICKS, CB), jnp.float32))
    operands = (mask, own, total, late, f34, *extra)
    return pl.pallas_call(
        functools.partial(finish_kernel, number, last),
        out_shape=out_shape,
        in_specs=[smem] + [vmem] * len(operands),
        out_specs=[vmem] * len(out_shape),
        compiler_params=pltpu.CompilerParams(vmem_limit_bytes=16 << 20),
        cost_estimate=pl.CostEstimate(
            flops=6 * TILE**3, bytes_accessed=1 << 20, transcendentals=0
        ),
        name="square_last" if last else "square",
    )(branches, *operands)


def move(value, route):
    return lax.ppermute(value, AXES, route)


def gather_rows(own):
    first = jnp.stack([own] + [move(own, first_leg(hops)) for hops in (1, 2, 3)])
    return [first] + [move(first, second_leg(hops)) for hops in (1, 2, 3)]


def gather_columns(own, first):
    own_swap = move(own, other_core())
    pair = jnp.stack([own, own_swap])
    n1 = move(pair, along_z(1))
    n2 = move(pair, along_z(2))
    later, _, _ = lax.optimization_barrier((n2, n1, first))
    n3 = move(later, along_z(1))
    n4 = move(later[0], along_z(2))
    near, _ = lax.optimization_barrier((jnp.concatenate([n1, n2]), n4))
    f12 = move(near, other_core())
    f34 = move(jnp.concatenate([n3, n4[None]]), other_core())
    return [own_swap, n1, n2, n3, n4, f12, f34]


def on_device(density, pattern, branches, basis, brick_list):
    row = lax.axis_index("row")
    col = lax.axis_index("col")
    layer = lax.axis_index("layer")
    place = jnp.stack([row // 2, row % 2, col, layer]).astype(jnp.int32)
    own = lax.dynamic_slice_in_dim(density, layer * TILE, TILE, 1)
    panel = col * NY + layer
    blocks = lax.dynamic_slice(
        pattern, (row * (TILE // DB), panel * (TILE // DB)), (TILE // DB, TILE // DB)
    )
    mask = jnp.repeat(jnp.repeat(blocks.astype(jnp.bfloat16), DB, 0), DB, 1)
    owners = jnp.tile(brick_list, (1, DB // brick_list.shape[1])).reshape(-1)
    extra = (
        lax.dynamic_slice_in_dim(owners, row * TILE, TILE, 0)[:, None],
        lax.dynamic_slice_in_dim(owners, panel * TILE, TILE, 0)[None, :],
        lax.dynamic_slice_in_dim(basis, row * TILE, TILE, 0),
        lax.dynamic_slice_in_dim(basis, panel * TILE, TILE, 0),
    )
    for number in range(STEPS):
        last = number == STEPS - 1
        rows = gather_rows(own)
        out = run_step(
            number, last, place, branches, mask, own, rows, gather_columns(own, rows[0]),
            extra if last else (),
        )
        own = out[0]
    shifted = [lax.ppermute(own, "layer", [(y, (y + hops) % NY) for y in range(NY)]) for hops in (1, 2, 3)]
    purified = join_layers(place, [own] + shifted)
    bricks = out[1].reshape(PANELS, PANELS, CB)
    bricks = lax.all_to_all(bricks, "row", 0, 0).sum(0)
    bricks = lax.all_to_all(bricks, ("col", "layer"), 0, 0, tiled=True).sum(0)
    return (purified, bricks.reshape(1, 1, 1, -1))


def solution(mesh):
    placed = (P("row", "col"), P(), P(), P(), P())
    return jax.shard_map(
        on_device,
        mesh=mesh,
        in_specs=placed,
        out_specs=(P("row", "col"), P("row", "col", "layer", None)),
        check_vma=False,
    )
```
